1024 devices in a mesh: dp: 8 (over y), ctx: 16 (over z), tp: 8 (over x, core).
Axes of the slice: x: 4, y: 8, z: 16, core: 2. Of those that a mesh axis runs over, the one named last changes fastest.
Arguments:
- tokens: bfloat16 [16384, 4096], P(('dp', 'ctx'), 'tp'), parts along dimension 0, may hold values from -6 to 6
- expert_ids: int32 [16384, 8], P(('dp', 'ctx')), parts along dimension 0, may hold values from 0 to 127, all different within a row; in each aligned block of 128 rows (0 to 127, 128 to 255, ...) at most 16 rows name the same one
- route_weight: float32 [16384, 8], P(('dp', 'ctx')), parts along dimension 0, may hold values from 0.1 to 1
- gate_weight: bfloat16 [128, 384, 4096], P(('ctx', 'tp')), may hold values from -0.09375 to 0.09375
- up_weight: bfloat16 [128, 384, 4096], P(('ctx', 'tp')), may hold values from -0.09375 to 0.09375
- down_weight: bfloat16 [128, 384, 4096], P(('ctx', 'tp')), may hold values from -0.15625 to 0.15625
Outputs:
- mixed_out: bfloat16 [16384, 4096], P(('dp', 'ctx'), 'tp'), parts along dimension 0
The draws below stay inside these ranges and needn't reach their ends.
There are 8 independent parts, one for each index of `dp`. The reference program is written for one: setup_inputs(seed, part) draws one part's arguments, and reference() takes and returns one part's arrays. A program takes and returns all parts, laid end to end along the dimension named above; an argument that names none is the same for every part. Nothing has to cross between parts.
Inputs may be any that keep to these rules, and one draw needn't show every extreme that they name: `expert_ids`: each token names 8 different experts. In each aligned block of 128 tokens no expert is named by more than 16 tokens, a bound that some block reaches.
All inputs are finite; a program needn't handle non-finite values.
Results may differ from the reference program's by a relative error of at most 0.018.
Values may be sent and summed in bfloat16 or wider, within the bound.
A program may use at most 128 MiB of HBM per device.

```python
import math
import jax
import jax.numpy as jnp
import numpy as np
from jax import lax

D = 4096
FF = 1536
EXPERTS = 128
TOP = 8
SPLIT = 4
TOK_CTX = 128
EXP_WIN = 32
CAP = 16
TOKENS = 2048
N_CTX = 16


def steps_of(rng, shape, cuts, low, high):
    loudness = 1.0
    for dim, parts in cuts:
        steps = jax.random.uniform(jax.random.fold_in(jax.random.fold_in(rng, 6), dim), (parts,), jnp.float32, low / len(cuts), high / len(cuts))
        loudness = loudness * jnp.repeat(jnp.exp(steps), shape[dim] // parts).reshape((-1,) + (1,) * (len(shape) - 1 - dim))
    return loudness


def routed_block(own_key, own, number, rows, number_of, top, bound, skew):
    sequence = jax.random.permutation(own_key, number_of)
    crowded, usual = portions_of(number_of, rows * top, bound, skew, True), portions_of(number_of, rows * top, bound, skew, False)
    places = jnp.arange(number_of)

    def named(sizes, rotation):
        used = int((sizes > 0).sum())
        fixed = max(1, used // 4)
        passed = fixed + (places - fixed + rotation * (used - fixed)) % max(1, number_of - fixed)
        return jnp.zeros((number_of,), jnp.int32).at[sequence[jnp.where(places < fixed, places, passed)]].set(jnp.asarray(sizes, jnp.int32))

    sizes = jnp.where(number % 4 == 0, named(crowded, number // 4), named(usual, number - number // 4 - 1))
    mixed = jax.random.permutation(jax.random.fold_in(own, 3), number_of)
    giver, sink = mixed[0:number_of // 2 * 2:2], mixed[1:number_of // 2 * 2:2]
    room = jnp.minimum(sizes[giver] - 1, bound - sizes[sink]) // 2
    room = jnp.where((giver == sequence[0]) | (sink == sequence[0]) | (sizes[sink] == 0), 0, jnp.maximum(room, 0))
    passed = jax.random.randint(jax.random.fold_in(own, 4), (number_of // 2,), 0, 1 << 20) % (room + 1)
    sizes = sizes.at[giver].add(-passed).at[sink].add(passed)
    labels = jnp.searchsorted(jnp.cumsum(sizes), jnp.arange(rows * top), side="right").astype(jnp.int32)
    table = labels.reshape(top, rows).T
    table = table[jax.random.permutation(jax.random.fold_in(own, 1), rows)]
    rotation = jax.random.randint(jax.random.fold_in(own, 2), (rows, 1), 0, top)
    return jnp.take_along_axis(table, (jnp.arange(top)[None, :] + rotation) % top, axis=1)


def portions_of(amount, total, reach, skew, full):
    loads = [(1 << 20) // math.isqrt(standing ** skew) + 1 for standing in range(1, amount + 1)]
    largest = reach if full else min(reach, max(-(-total // amount), total * loads[0] // sum(loads)))
    least = 1 if total - largest >= amount - 1 else 0
    given, surplus = [largest] + [least] * (amount - 1), total - largest - least * (amount - 1)
    while surplus > 0:
        candidates = [i for i in range(1, amount) if given[i] < largest] or [i for i in range(1, amount) if given[i] < reach]
        whole, left = sum([loads[i] for i in candidates]), surplus
        for i in candidates:
            extra = min(reach - given[i], max(1, left * loads[i] // whole), surplus)
            given[i] = given[i] + extra
            surplus = surplus - extra
    return np.array(given)


def normal_values(rng, shape, deviation, limit, split=(), kind=jnp.bfloat16):
    array = deviation * jax.random.normal(rng, shape, jnp.float32)
    if split:
        array = array * steps_of(rng, shape, split, -0.22, 0.18)
    return jnp.clip(array, -limit, limit).astype(kind)


def setup_inputs(seed: int = 0, part: int = 0) -> dict:
    streams_of = jax.random.split(jax.random.key(seed), 7)
    part_splits = jax.random.split(jax.random.fold_in(streams_of[6], part), 7)
    tokens = normal_values(part_splits[0], (TOKENS, D), 1.0, 6.0, ((0, 16), (1, 8)))
    expert_ids_keys = jax.random.split(jax.random.fold_in(part_splits[1], 1), TOKENS // TOK_CTX)
    expert_ids_turns = jax.random.permutation(jax.random.fold_in(part_splits[1], 3), TOKENS // TOK_CTX)
    expert_ids = jax.vmap(lambda own, number: routed_block(jax.random.fold_in(part_splits[1], 2), own, number, TOK_CTX, EXPERTS, TOP, CAP, 2))(expert_ids_keys, expert_ids_turns).reshape((TOKENS, TOP))
    route_weight = jnp.clip(jnp.exp(math.log(1.0) - 2.3025851 * jax.random.uniform(part_splits[2], (TOKENS, TOP), jnp.float32) ** steps_of(part_splits[2], (TOKENS, TOP), ((0, 16),), -0.2, 0.2)), 0.1, 1.0)
    gate_weight = normal_values(streams_of[3], (EXP_WIN * SPLIT, FF // SPLIT, D), D ** -0.5, 0.09375, ((0, 128),))
    up_weight = normal_values(streams_of[4], (EXP_WIN * SPLIT, FF // SPLIT, D), D ** -0.5, 0.09375, ((0, 128),))
    down_weight = normal_values(streams_of[5], (EXP_WIN * SPLIT, FF // SPLIT, D), FF ** -0.5, 0.15625, ((0, 128),))
    return {"tokens": tokens, "expert_ids": expert_ids, "route_weight": route_weight, "gate_weight": gate_weight, "up_weight": up_weight, "down_weight": down_weight}


def plan(block_ids):
    flat_ids = block_ids.reshape(-1)
    live_route = flat_ids < EXP_WIN
    expert_marks = (flat_ids[:, None] == jnp.arange(EXP_WIN, dtype=jnp.int32)[None, :]).astype(jnp.int32)
    running = jnp.cumsum(expert_marks, axis=0, dtype=jnp.int32) - 1
    slot_index = jnp.sum(running * expert_marks, axis=1, dtype=jnp.int32)
    target_row = jnp.where(live_route, flat_ids * CAP + slot_index, -1).astype(jnp.int32)
    place_index = jnp.arange(EXP_WIN * CAP, dtype=jnp.int32)
    select_mask = (target_row[None, :] == place_index[:, None]).astype(jnp.float32)
    return select_mask.reshape(EXP_WIN * CAP, TOK_CTX, TOP)


def expert_pass(pieces):
    rows, gate_w, up_w, down_w = pieces
    gate_vals = jnp.dot(rows, gate_w.T, preferred_element_type=jnp.float32)
    up_vals = jnp.dot(rows, up_w.T, preferred_element_type=jnp.float32)
    hidden = (jax.nn.silu(gate_vals) * up_vals).astype(jnp.bfloat16)
    quarters = hidden.reshape(rows.shape[0], SPLIT, FF // SPLIT).astype(jnp.float32)
    down_parts = down_w.reshape(SPLIT, FF // SPLIT, D).astype(jnp.float32)
    part_out = jnp.einsum("rqf,qfd->qrd", quarters, down_parts,
                          precision=lax.Precision.HIGHEST).astype(jnp.bfloat16)
    return jnp.sum(part_out.astype(jnp.float32), axis=0)


def reference(tokens, expert_ids, route_weight, gate_weight, up_weight, down_weight):
    gate_full = gate_weight.reshape(EXP_WIN, FF, D)
    up_full = up_weight.reshape(EXP_WIN, FF, D)
    down_full = down_weight.reshape(EXP_WIN, FF, D)
    block_tokens = tokens.reshape(N_CTX, TOK_CTX, D)
    block_ids = expert_ids.reshape(N_CTX, TOK_CTX, TOP)
    block_weight = route_weight.reshape(N_CTX, TOK_CTX, TOP)
    masks = jax.vmap(plan)(block_ids)
    pick_matrix = jnp.sum(masks, axis=3)
    outgoing = jnp.einsum("bpt,btd->bpd", pick_matrix, block_tokens.astype(jnp.float32),
                          precision=lax.Precision.HIGHEST).astype(jnp.bfloat16)
    arranged = outgoing.reshape(N_CTX, EXP_WIN, CAP, D).transpose(1, 0, 2, 3).reshape(EXP_WIN, N_CTX * CAP, D)
    expert_sum = lax.map(expert_pass, (arranged, gate_full, up_full, down_full))
    expert_sum = expert_sum.reshape(EXP_WIN, N_CTX, CAP, D).transpose(1, 0, 2, 3).reshape(N_CTX, EXP_WIN * CAP, D)
    combine = jnp.sum(masks * block_weight[:, None, :, :], axis=3)
    mixed_out = jnp.einsum("bpt,bpd->btd", combine, expert_sum,
                           precision=lax.Precision.HIGHEST)
    return mixed_out.astype(jnp.bfloat16).reshape(TOKENS, D)
```

```python
import jax
import jax.numpy as jnp
from jax import lax
from jax.experimental import pallas as pl
from jax.experimental.pallas import tpu as pltpu
from jax.sharding import PartitionSpec as P

MESH = pl.DeviceIdType.MESH
N = 16
CAP = 16
TOK = 128
TOP = 8
FS = 512
NS = 8
FQ = 384
NCH = 4
CB = N // NCH
CR = CB * CAP
DIST = [8, 7, 9, 6, 10, 5, 11, 4, 12, 3, 13, 2, 14, 1, 15, 0]
POS = {d: p for p, d in enumerate(DIST)}
BACK = [POS[(-d) % N] for d in DIST]


def kernel(tok, ids, rw, gate_h, up_h, down_h, out,
           xs, gate_v, up_v, down_v, pk, comb_hi, comb_lo, back, own, mate_s, mate_r, pair_s, pair_r, ret,
           wsem, zs, zr, xsend, xrecv, ms, mr, ps, pr, rs, rr):
    dp, c, t = lax.axis_index("dp"), lax.axis_index("ctx"), lax.axis_index("tp")
    x, k = t // 2, t % 2
    x2 = 3 - x
    xp = x + 1 - 2 * (x % 2)
    xp2 = 3 - xp
    t2 = 2 * x2 + k
    group = x // 2
    mate = 2 * x + 1 - k
    pair_same, pair_other = 2 * xp + k, 2 * xp + 1 - k

    def ctx_of(d):
        return lax.rem(c + d, N)

    def dev(cc, tt):
        return (dp, cc, tt)

    wcopies = [pltpu.make_async_copy(h, v, wsem.at[i])
               for i, (h, v) in enumerate(((gate_h, gate_v), (up_h, up_v), (down_h, down_v)))]
    for w in wcopies:
        w.start()

    barrier = pltpu.get_barrier_semaphore()
    peers = [dev(ctx_of(d), tt) for d in range(1, N) for tt in (t, t2)]
    peers += [dev(c, tt) for tt in (t2, mate, pair_same, pair_other)]
    for peer in peers:
        pl.semaphore_signal(barrier, inc=1, device_id=peer, device_id_type=MESH)

    place = lax.broadcasted_iota(jnp.int32, (2 * N, TOK), 0)
    expert = jnp.zeros((2 * N, TOK), jnp.int32)
    for p, d in enumerate(DIST):
        base = 2 * ctx_of(d)
        expert = jnp.where(place == 2 * p, base + group, expert)
        expert = jnp.where(place == 2 * p + 1, base + 1 - group, expert)
    marks = jnp.zeros((2 * N, TOK), jnp.float32)
    weight = jnp.zeros((2 * N, TOK), jnp.float32)
    for j in range(TOP):
        hit = ids[j:j + 1, :] == expert
        marks = jnp.where(hit, 1.0, marks)
        weight = jnp.where(hit, rw[j:j + 1, :], weight)
    row = lax.broadcasted_iota(jnp.int32, (TOK, TOK), 0)
    col = lax.broadcasted_iota(jnp.int32, (TOK, TOK), 1)
    above = jnp.where(row < col, 1.0, 0.0).astype(jnp.bfloat16)
    count = jnp.dot(marks.astype(jnp.bfloat16), above, preferred_element_type=jnp.float32)
    slot = jnp.where(marks > 0.0, count, -1.0)
    numbers = lax.broadcasted_iota(jnp.int32, (2 * N, CAP, TOK), 1).astype(jnp.float32)
    chosen = slot[:, None, :] == numbers
    pick = jnp.where(chosen, 1.0, 0.0).reshape(2 * N * CAP, TOK).astype(jnp.bfloat16)
    pk[...] = jnp.dot(pick, tok[...], preferred_element_type=jnp.float32).astype(jnp.bfloat16)

    pl.semaphore_wait(barrier, len(peers))

    def remote(src, dst, ssem, rsem, to):
        return pltpu.make_async_remote_copy(src_ref=src, dst_ref=dst, send_sem=ssem, recv_sem=rsem,
                                            device_id=to, device_id_type=MESH)

    pending = []

    for p, d in enumerate(DIST):
        q = BACK[p]
        for g, tt in ((0, t), (1, t2)):
            src = pk.at[pl.ds((2 * p + g) * CAP, CAP)]
            if d == 0 and g == 0:
                xs[t, q * CAP:(q + 1) * CAP, :] = src[...]
                continue
            cp = remote(src, xs.at[t, pl.ds(q * CAP, CAP)], zs.at[2 * p + g], zr.at[2 * q + g], dev(ctx_of(d), tt))
            cp.start()
            pending.append(cp)

    comb = jnp.where(chosen, weight[:, None, :], 0.0).reshape(2 * N * CAP, TOK).T
    hi = comb.astype(jnp.bfloat16)
    comb_hi[...] = hi
    comb_lo[...] = (comb - hi.astype(jnp.float32)).astype(jnp.bfloat16)

    def stage_a(j):
        rows = pl.ds(j * CR, CR)
        for p in range(j * CB, (j + 1) * CB):
            for g in range(2):
                if DIST[p] == 0 and g == 0:
                    continue
                dst = xs.at[t if g == 0 else t2, pl.ds(p * CAP, CAP)]
                remote(dst, dst, zs.at[2 * p + g], zr.at[2 * p + g], dev(c, mate)).wait_recv()
        for i, to in enumerate((pair_same, pair_other, mate)):
            for g, tt in ((0, t), (1, t2)):
                cp = remote(xs.at[tt, rows], xs.at[tt, rows], xsend.at[j, 2 * i + g], xrecv.at[j, 2 * i + g], dev(c, to))
                cp.start()
                pending.append(cp)

    def stage_b(j):
        rows = pl.ds(j * CR, CR)
        froms = ((2 * xp + k, 2 * xp2 + k), (2 * xp + 1 - k, 2 * xp2 + 1 - k), (2 * x + 1 - k, 2 * x2 + 1 - k))
        for i, slices in enumerate(froms):
            for g in range(2):
                dst = xs.at[slices[g], rows]
                remote(dst, dst, xsend.at[j, 2 * i + g], xrecv.at[j, 2 * i + g], dev(c, mate)).wait_recv()
        if j == 0:
            wcopies[0].wait()
            wcopies[1].wait()

        def gate_up(s, accs):
            g_acc, u_acc = accs
            a = xs[s, rows, :]
            cols = pl.ds(pl.multiple_of(s * FS, FS), FS)
            nt = (((1,), (1,)), ((), ()))
            g_acc = g_acc + lax.dot_general(a, gate_v[:, cols], nt, preferred_element_type=jnp.float32)
            u_acc = u_acc + lax.dot_general(a, up_v[:, cols], nt, preferred_element_type=jnp.float32)
            return g_acc, u_acc

        zero = jnp.zeros((CR, FQ), jnp.float32)
        g_acc, u_acc = lax.fori_loop(0, NS, gate_up, (zero, zero))
        hidden = (g_acc / (1.0 + jnp.exp(-g_acc)) * u_acc).astype(jnp.bfloat16)
        if j == 0:
            wcopies[2].wait()

        def down(s):
            cols = pl.ds(pl.multiple_of(s * FS, FS), FS)
            return jnp.dot(hidden, down_v[:, cols], preferred_element_type=jnp.float32)

        for xq in range(4):
            mate_s[j, xq] = down(2 * xq + 1 - k).astype(jnp.bfloat16)
        cp = remote(mate_s.at[j], mate_r.at[j], ms.at[j], mr.at[j], dev(c, mate))
        cp.start()
        pending.append(cp)
        for i, xq in enumerate((x, x2, xp, xp2)):
            own[j, i] = down(2 * xq + k)

    def stage_c(j):
        remote(mate_s.at[j], mate_r.at[j], ms.at[j], mr.at[j], dev(c, mate)).wait_recv()
        for i, xq in enumerate((xp, xp2)):
            pair_s[j, i] = (own[j, 2 + i] + mate_r[j, xq].astype(jnp.float32)).astype(jnp.bfloat16)
        cp = remote(pair_s.at[j], pair_r.at[j], ps.at[j], pr.at[j], dev(c, pair_same))
        cp.start()
        pending.append(cp)
        for i, xq in enumerate((x, x2)):
            own[j, i] = own[j, i] + mate_r[j, xq].astype(jnp.float32)

    def stage_d(j):
        remote(pair_s.at[j], pair_r.at[j], ps.at[j], pr.at[j], dev(c, pair_same)).wait_recv()
        for i in range(2):
            ret[j, i] = (own[j, i] + pair_r[j, i].astype(jnp.float32)).astype(jnp.bfloat16)
        for b in range(CB):
            p = j * CB + b
            q = BACK[p]
            for g, tt in ((0, t), (1, t2)):
                src = ret.at[j, g, pl.ds(b * CAP, CAP)]
                if DIST[p] == 0 and g == 0:
                    back[2 * q * CAP:(2 * q + 1) * CAP, :] = src[...]
                    continue
                cp = remote(src, back.at[pl.ds((2 * q + g) * CAP, CAP)], rs.at[2 * p + g], rr.at[2 * q + g],
                            dev(ctx_of(DIST[p]), tt))
                cp.start()
                pending.append(cp)

    for n in range(NCH + 3):
        if n < NCH:
            stage_a(n)
        if 0 <= n - 1 < NCH:
            stage_b(n - 1)
        if 0 <= n - 2 < NCH:
            stage_c(n - 2)
        if 0 <= n - 3 < NCH:
            stage_d(n - 3)

    total = None
    for j in range(NCH):
        for p in range(j * CB, (j + 1) * CB):
            for g in range(2):
                if DIST[p] == 0 and g == 0:
                    continue
                dst = back.at[pl.ds((2 * p + g) * CAP, CAP)]
                remote(dst, dst, rs.at[2 * p + g], rr.at[2 * p + g], dev(c, mate)).wait_recv()
        cols = slice(2 * j * CR, 2 * (j + 1) * CR)
        piece = back[cols, :]
        part = (jnp.dot(comb_hi[:, cols], piece, preferred_element_type=jnp.float32)
                + jnp.dot(comb_lo[:, cols], piece, preferred_element_type=jnp.float32))
        total = part if total is None else total + part
    out[...] = total.astype(jnp.bfloat16)
    for cp in pending:
        cp.wait_send()


def shards(tokens, expert_ids, route_weight, gate_weight, up_weight, down_weight):
    bf, f32 = jnp.bfloat16, jnp.float32
    vmem, dma = pltpu.VMEM, pltpu.SemaphoreType.DMA
    full = pl.BlockSpec(memory_space=pltpu.VMEM)
    hbm = pl.BlockSpec(memory_space=pl.ANY)
    return pl.pallas_call(
        kernel,
        out_shape=jax.ShapeDtypeStruct((TOK, FS), bf),
        in_specs=[full, full, full, hbm, hbm, hbm],
        out_specs=full,
        scratch_shapes=[
            vmem((NS, N * CAP, FS), bf),
            vmem((FQ, NS * FS), bf), vmem((FQ, NS * FS), bf), vmem((FQ, NS * FS), bf),
            vmem((2 * N * CAP, FS), bf), vmem((TOK, 2 * N * CAP), bf), vmem((TOK, 2 * N * CAP), bf),
            vmem((2 * N * CAP, FS), bf),
            vmem((NCH, 4, CR, FS), f32),
            vmem((NCH, 4, CR, FS), bf), vmem((NCH, 4, CR, FS), bf),
            vmem((NCH, 2, CR, FS), bf), vmem((NCH, 2, CR, FS), bf),
            vmem((NCH, 2, CR, FS), bf),
            dma((3,)), dma((2 * N,)), dma((2 * N,)), dma((NCH, 6)), dma((NCH, 6)),
            dma((NCH,)), dma((NCH,)), dma((NCH,)), dma((NCH,)), dma((2 * N,)), dma((2 * N,)),
        ],
        compiler_params=pltpu.CompilerParams(collective_id=0, has_side_effects=True, vmem_limit_bytes=60 << 20),
    )(tokens, expert_ids.T, route_weight.T, gate_weight[0], up_weight[0], down_weight[0])


def solution(mesh):
    return jax.shard_map(
        shards,
        mesh=mesh,
        in_specs=(
            P(("dp", "ctx"), "tp"),
            P(("dp", "ctx"), None),
            P(("dp", "ctx"), None),
            P(("ctx", "tp"), None, None),
            P(("ctx", "tp"), None, None),
            P(("ctx", "tp"), None, None),
        ),
        out_specs=P(("dp", "ctx"), "tp"),
        check_vma=False,
    )
```

```python
import jax
import jax.numpy as jnp
from jax import lax
from jax.experimental import pallas as pl
from jax.experimental.pallas import tpu as pltpu
from jax.sharding import PartitionSpec as P

MESH = pl.DeviceIdType.MESH
N = 16
CAP = 16
TOK = 128
TOP = 8
FS = 512
NS = 8
NX = 4
FQ = 384
SIZES = [4, 4, 4, 2, 2]
NCH = len(SIZES)
STARTS = [sum(SIZES[:j]) for j in range(NCH)]
DIST = [0, 8, 1, 15, 2, 14, 7, 9, 3, 13, 6, 10, 4, 12, 5, 11]
ORDER = ("A0", "S2", "A1", "S3", "F0", "B0", "F1", "C0", "A2", "S4", "B1", "D0",
         "A3", "F2", "C1", "B2", "D1", "A4", "F3", "C2", "B3", "D2", "F4", "C3",
         "B4", "D3", "C4", "D4")
POS = {d: p for p, d in enumerate(DIST)}
BACK = [POS[(-d) % N] for d in DIST]


def kernel(tok_h, ids_h, rw_h, gate_h, up_h, down_h, out,
           tok, ids, rw, zin, xs, gate_v, up_v, down_v, pk, comb_hi, comb_lo, back, own, mate_s, mate_r, chip_s, chip_r, ret,
           wsem, zs, zr, xsend, xrecv, fs, fr, ms, mr, ps, pr, rs, rr):
    dp, c, t = lax.axis_index("dp"), lax.axis_index("ctx"), lax.axis_index("tp")
    x, k = t // 2, t % 2
    group = t // 4
    mate = 2 * x + 1 - k

    def ctx_of(d):
        return lax.rem(c + d, N)

    def dev(cc, tt):
        return (dp, cc, tt)

    def chip(o):
        return lax.rem(x + o, NX)

    def local(h, v, i):
        return pltpu.make_async_copy(h, v, wsem.at[i])

    icopies = [local(ids_h, ids, 3), local(rw_h, rw, 4), local(tok_h, tok, 5)]
    for w in icopies:
        w.start()
    wcopies = [local(gate_h, gate_v, 0), local(up_h, up_v, 1), local(down_h, down_v, 2)]

    barrier = pltpu.get_barrier_semaphore()
    peers = [dev(ctx_of(d), t) for d in range(1, N)] + [dev(c, 2 * chip(o) + k) for o in range(1, NX)] + [dev(c, mate)]
    for peer in peers:
        pl.semaphore_signal(barrier, inc=1, device_id=peer, device_id_type=MESH)

    for w in icopies:
        w.wait()

    place = lax.broadcasted_iota(jnp.int32, (2 * N, TOK), 0)
    expert = jnp.zeros((2 * N, TOK), jnp.int32)
    for p, d in enumerate(DIST):
        expert = jnp.where(place == p, 2 * ctx_of(d), expert)
        expert = jnp.where(place == N + p, 2 * ctx_of(d) + 1, expert)
    marks = jnp.zeros((2 * N, TOK), jnp.float32)
    weight = jnp.zeros((2 * N, TOK), jnp.float32)
    for j in range(TOP):
        hit = ids[j:j + 1, :] == expert
        marks = jnp.where(hit, 1.0, marks)
        weight = jnp.where(hit, rw[j:j + 1, :], weight)
    row = lax.broadcasted_iota(jnp.int32, (TOK, TOK), 0)
    col = lax.broadcasted_iota(jnp.int32, (TOK, TOK), 1)
    above = jnp.where(row < col, 1.0, 0.0).astype(jnp.bfloat16)
    count = jnp.dot(marks.astype(jnp.bfloat16), above, preferred_element_type=jnp.float32)
    slot = jnp.where(marks > 0.0, count, -1.0)
    numbers = lax.broadcasted_iota(jnp.int32, (2 * N, CAP, TOK), 1).astype(jnp.float32)
    chosen = slot[:, None, :] == numbers

    def rows_of(j):
        return pl.ds(STARTS[j] * CAP, SIZES[j] * CAP)

    def blocks_of(j):
        return range(STARTS[j], STARTS[j] + SIZES[j])

    def pack(j):
        for g in range(2):
            first = g * N + STARTS[j]
            pick = jnp.where(chosen[first:first + SIZES[j]], 1.0, 0.0).reshape(SIZES[j] * CAP, TOK).astype(jnp.bfloat16)
            pk[g, rows_of(j), :] = jnp.dot(pick, tok[...], preferred_element_type=jnp.float32).astype(jnp.bfloat16)

    pack(0)
    pl.semaphore_wait(barrier, len(peers))

    def remote(src, dst, ssem, rsem, to):
        return pltpu.make_async_remote_copy(src_ref=src, dst_ref=dst, send_sem=ssem, recv_sem=rsem,
                                            device_id=to, device_id_type=MESH)

    pending = []

    def dispatch(j):
        for p in blocks_of(j):
            q, d = BACK[p], DIST[p]
            src, dst = pk.at[:, pl.ds(p * CAP, CAP)], zin.at[:, pl.ds(q * CAP, CAP)]
            if d == 0:
                dst[...] = src[...]
                continue
            cp = remote(src, dst, zs.at[p], zr.at[q], dev(ctx_of(d), t))
            cp.start()
            pending.append(cp)

    dispatch(0)
    pack(1)
    dispatch(1)
    for w in wcopies:
        w.start()
    for j in range(2, NCH):
        pack(j)
    comb = jnp.where(chosen, weight[:, None, :], 0.0).reshape(2 * N * CAP, TOK).T
    hi = comb.astype(jnp.bfloat16)
    comb_hi[...] = hi
    comb_lo[...] = (comb - hi.astype(jnp.float32)).astype(jnp.bfloat16)

    def stage_a(j):
        rows = rows_of(j)
        for p in blocks_of(j):
            if DIST[p] != 0:
                dst = zin.at[:, pl.ds(p * CAP, CAP)]
                remote(dst, dst, zs.at[p], zr.at[p], dev(ctx_of(1), t)).wait_recv()
        for o in (2, 1, 3):
            to = chip(o)
            cp = remote(zin.at[to // 2, rows], xs.at[k, x, rows], xsend.at[j, o], xrecv.at[j, o], dev(c, 2 * to + k))
            cp.start()
            pending.append(cp)
        xs[k, x, rows, :] = zin[group, rows, :]

    def stage_f(j):
        rows = rows_of(j)
        for o in (1, 3, 2):
            dst = xs.at[k, chip(NX - o), rows]
            remote(dst, dst, xsend.at[j, o], xrecv.at[j, o], dev(c, mate)).wait_recv()
        cp = remote(xs.at[k, :, rows], xs.at[k, :, rows], fs.at[j], fr.at[j], dev(c, mate))
        cp.start()
        pending.append(cp)

    def stage_b(j):
        rows = rows_of(j)
        if j == 0:
            wcopies[0].wait()
            wcopies[1].wait()

        def gate_up(parity):
            g_acc = u_acc = None
            nt = (((1,), (1,)), ((), ()))
            for xq in range(NX):
                a = xs[parity, xq, rows, :]
                cols = pl.ds(pl.multiple_of((2 * xq + parity) * FS, FS), FS)
                g_new = lax.dot_general(a, gate_v[:, cols], nt, preferred_element_type=jnp.float32)
                u_new = lax.dot_general(a, up_v[:, cols], nt, preferred_element_type=jnp.float32)
                g_acc = g_new if g_acc is None else g_acc + g_new
                u_acc = u_new if u_acc is None else u_acc + u_new
            return g_acc, u_acc

        g_mine, u_mine = gate_up(k)
        dst = xs.at[1 - k, :, rows]
        remote(dst, dst, fs.at[j], fr.at[j], dev(c, mate)).wait_recv()
        g_mate, u_mate = gate_up(1 - k)
        g_acc, u_acc = g_mine + g_mate, u_mine + u_mate
        hidden = (g_acc / (1.0 + jnp.exp(-g_acc)) * u_acc).astype(jnp.bfloat16)
        if j == 0:
            wcopies[2].wait()

        def down(xq, parity):
            cols = pl.ds(pl.multiple_of((2 * xq + parity) * FS, FS), FS)
            return jnp.dot(hidden, down_v[:, cols], preferred_element_type=jnp.float32)

        for xq in range(NX):
            mate_s[xq, rows, :] = down(xq, 1 - k).astype(jnp.bfloat16)
        cp = remote(mate_s.at[:, rows], mate_r.at[:, rows], ms.at[j], mr.at[j], dev(c, mate))
        cp.start()
        pending.append(cp)
        for o in range(NX):
            own[o, rows, :] = down(chip(o), k)

    def stage_c(j):
        rows = rows_of(j)
        remote(mate_s.at[:, rows], mate_r.at[:, rows], ms.at[j], mr.at[j], dev(c, mate)).wait_recv()
        for o in (2, 1, 3):
            to = chip(o)
            chip_s[o, rows, :] = (own[o, rows, :] + mate_r[to, rows, :].astype(jnp.float32)).astype(jnp.bfloat16)
            cp = remote(chip_s.at[o, rows], chip_r.at[x, rows], ps.at[j, o], pr.at[j, o], dev(c, 2 * to + k))
            cp.start()
            pending.append(cp)
        own[0, rows, :] = own[0, rows, :] + mate_r[x, rows, :].astype(jnp.float32)

    def stage_d(j):
        rows = rows_of(j)
        for o in (1, 3, 2):
            dst = chip_r.at[chip(NX - o), rows]
            remote(dst, dst, ps.at[j, o], pr.at[j, o], dev(c, mate)).wait_recv()
        pair = x + 1 - 2 * (x % 2)
        far = 2 * (1 - group)
        ret[group, rows, :] = (own[0, rows, :] + chip_r[pair, rows, :].astype(jnp.float32)).astype(jnp.bfloat16)
        ret[1 - group, rows, :] = (chip_r[far, rows, :].astype(jnp.float32)
                                   + chip_r[far + 1, rows, :].astype(jnp.float32)).astype(jnp.bfloat16)
        for p in blocks_of(j):
            q, d = BACK[p], DIST[p]
            src, dst = ret.at[:, pl.ds(p * CAP, CAP)], back.at[:, pl.ds(q * CAP, CAP)]
            if d == 0:
                dst[...] = src[...]
                continue
            cp = remote(src, dst, rs.at[p], rr.at[q], dev(ctx_of(d), t))
            cp.start()
            pending.append(cp)

    stages = {"A": stage_a, "F": stage_f, "B": stage_b, "C": stage_c, "D": stage_d, "S": dispatch}
    for step in ORDER:
        stages[step[0]](int(step[1]))

    total = None
    half = N // 2
    for h in range(2):
        for p in range(h * half, (h + 1) * half):
            if DIST[p] != 0:
                dst = back.at[:, pl.ds(p * CAP, CAP)]
                remote(dst, dst, rs.at[p], rr.at[p], dev(ctx_of(1), t)).wait_recv()
        for g in range(2):
            piece = back[g, h * half * CAP:(h + 1) * half * CAP, :]
            first = g * N * CAP + h * half * CAP
            cols = slice(first, first + half * CAP)
            part = (jnp.dot(comb_hi[:, cols], piece, preferred_element_type=jnp.float32)
                    + jnp.dot(comb_lo[:, cols], piece, preferred_element_type=jnp.float32))
            total = part if total is None else total + part
    out[...] = total.astype(jnp.bfloat16)
    for cp in pending:
        cp.wait_send()


def shards(tokens, expert_ids, route_weight, gate_weight, up_weight, down_weight):
    bf, f32 = jnp.bfloat16, jnp.float32
    vmem, dma = pltpu.VMEM, pltpu.SemaphoreType.DMA
    full = pl.BlockSpec(memory_space=pltpu.VMEM)
    hbm = pl.BlockSpec(memory_space=pltpu.HBM)
    return pl.pallas_call(
        kernel,
        out_shape=jax.ShapeDtypeStruct((TOK, FS), bf),
        in_specs=[hbm] * 6,
        out_specs=full,
        scratch_shapes=[
            vmem((TOK, FS), bf), vmem((TOP, TOK), jnp.int32), vmem((TOP, TOK), f32),
            vmem((2, N * CAP, FS), bf), vmem((2, NX, N * CAP, FS), bf),
            vmem((FQ, NS * FS), bf), vmem((FQ, NS * FS), bf), vmem((FQ, NS * FS), bf),
            vmem((2, N * CAP, FS), bf), vmem((TOK, 2 * N * CAP), bf), vmem((TOK, 2 * N * CAP), bf),
            vmem((2, N * CAP, FS), bf),
            vmem((NX, N * CAP, FS), f32),
            vmem((NX, N * CAP, FS), bf), vmem((NX, N * CAP, FS), bf),
            vmem((NX, N * CAP, FS), bf), vmem((NX, N * CAP, FS), bf), vmem((2, N * CAP, FS), bf),
            dma((6,)), dma((N,)), dma((N,)), dma((NCH, NX)), dma((NCH, NX)), dma((NCH,)), dma((NCH,)),
            dma((NCH,)), dma((NCH,)), dma((NCH, NX)), dma((NCH, NX)), dma((N,)), dma((N,)),
        ],
        compiler_params=pltpu.CompilerParams(collective_id=0, has_side_effects=True, vmem_limit_bytes=60 << 20),
    )(tokens, expert_ids.T, route_weight.T, gate_weight[0], up_weight[0], down_weight[0])


def solution(mesh):
    return jax.shard_map(
        shards,
        mesh=mesh,
        in_specs=(
            P(("dp", "ctx"), "tp"),
            P(("dp", "ctx"), None),
            P(("dp", "ctx"), None),
            P(("ctx", "tp"), None, None),
            P(("ctx", "tp"), None, None),
            P(("ctx", "tp"), None, None),
        ),
        out_specs=P(("dp", "ctx"), "tp"),
        check_vma=False,
    )
```

```python
import jax
import jax.numpy as jnp
from jax import lax
from jax.experimental import pallas as pl
from jax.experimental.pallas import tpu as pltpu
from jax.sharding import PartitionSpec as P

MESH = pl.DeviceIdType.MESH
N = 16
CAP = 16
TOK = 128
TOP = 8
FS = 512
NS = 8
NX = 4
FQ = 384
SIZES = [4, 4, 4, 2, 2]
NCH = len(SIZES)
STARTS = [sum(SIZES[:j]) for j in range(NCH)]
DIST = [0, 8, 2, 14, 1, 15, 7, 9, 3, 13, 6, 10, 4, 12, 5, 11]
ORDER = ("A0", "S2", "X0", "A1", "S3", "X1", "F0", "B0", "F1", "C0", "A2", "S4",
         "X2", "B1", "D0", "A3", "X3", "F2", "C1", "B2", "D1", "A4", "X4", "F3",
         "C2", "B3", "D2", "F4", "C3", "B4", "D3", "C4", "D4")
POS = {d: p for p, d in enumerate(DIST)}
BACK = [POS[(-d) % N] for d in DIST]


def kernel(tok_h, ids_h, rw_h, gate_h, up_h, down_h, out,
           tok, ids, rw, zin, xs, gate_v, up_v, down_v, pk, comb_hi, comb_lo, back, own, mate_s, mate_r, chip_s, chip_r, ret,
           wsem, zs, zr, xsend, xrecv, fs, fr, ms, mr, ps, pr, rs, rr):
    dp, c, t = lax.axis_index("dp"), lax.axis_index("ctx"), lax.axis_index("tp")
    x, k = t // 2, t % 2
    group = t // 4
    mate = 2 * x + 1 - k

    def ctx_of(d):
        return lax.rem(c + d, N)

    def dev(cc, tt):
        return (dp, cc, tt)

    def chip(o):
        return lax.rem(x + o, NX)

    def local(h, v, i):
        return pltpu.make_async_copy(h, v, wsem.at[i])

    icopies = [local(ids_h, ids, 3), local(rw_h, rw, 4), local(tok_h, tok, 5)]
    for w in icopies:
        w.start()
    wcopies = [local(gate_h, gate_v, 0), local(up_h, up_v, 1), local(down_h, down_v, 2)]

    barrier = pltpu.get_barrier_semaphore()
    peers = [dev(ctx_of(d), t) for d in range(1, N)] + [dev(c, 2 * chip(o) + k) for o in range(1, NX)] + [dev(c, mate)]
    for peer in peers:
        pl.semaphore_signal(barrier, inc=1, device_id=peer, device_id_type=MESH)

    for w in icopies:
        w.wait()

    place = lax.broadcasted_iota(jnp.int32, (2 * N, TOK), 0)
    expert = jnp.zeros((2 * N, TOK), jnp.int32)
    for p, d in enumerate(DIST):
        expert = jnp.where(place == p, 2 * ctx_of(d), expert)
        expert = jnp.where(place == N + p, 2 * ctx_of(d) + 1, expert)
    marks = jnp.zeros((2 * N, TOK), jnp.float32)
    weight = jnp.zeros((2 * N, TOK), jnp.float32)
    for j in range(TOP):
        hit = ids[j:j + 1, :] == expert
        marks = jnp.where(hit, 1.0, marks)
        weight = jnp.where(hit, rw[j:j + 1, :], weight)
    row = lax.broadcasted_iota(jnp.int32, (TOK, TOK), 0)
    col = lax.broadcasted_iota(jnp.int32, (TOK, TOK), 1)
    above = jnp.where(row < col, 1.0, 0.0).astype(jnp.bfloat16)
    count = jnp.dot(marks.astype(jnp.bfloat16), above, preferred_element_type=jnp.float32)
    slot = jnp.where(marks > 0.0, count, -1.0)
    numbers = lax.broadcasted_iota(jnp.int32, (2 * N, CAP, TOK), 1).astype(jnp.float32)
    chosen = slot[:, None, :] == numbers

    def rows_of(j):
        return pl.ds(STARTS[j] * CAP, SIZES[j] * CAP)

    def blocks_of(j):
        return range(STARTS[j], STARTS[j] + SIZES[j])

    def pack(j):
        for g in range(2):
            first = g * N + STARTS[j]
            pick = jnp.where(chosen[first:first + SIZES[j]], 1.0, 0.0).reshape(SIZES[j] * CAP, TOK).astype(jnp.bfloat16)
            pk[g, rows_of(j), :] = jnp.dot(pick, tok[...], preferred_element_type=jnp.float32).astype(jnp.bfloat16)

    pack(0)
    pl.semaphore_wait(barrier, len(peers))

    def remote(src, dst, ssem, rsem, to):
        return pltpu.make_async_remote_copy(src_ref=src, dst_ref=dst, send_sem=ssem, recv_sem=rsem,
                                            device_id=to, device_id_type=MESH)

    pending = []

    def dispatch(j):
        for p in blocks_of(j):
            q, d = BACK[p], DIST[p]
            src, dst = pk.at[:, pl.ds(p * CAP, CAP)], zin.at[:, pl.ds(q * CAP, CAP)]
            if d == 0:
                dst[...] = src[...]
                continue
            cp = remote(src, dst, zs.at[p], zr.at[q], dev(ctx_of(d), t))
            cp.start()
            pending.append(cp)

    dispatch(0)
    pack(1)
    dispatch(1)
    for w in wcopies:
        w.start()
    for j in range(2, NCH):
        pack(j)
    comb = jnp.where(chosen, weight[:, None, :], 0.0).reshape(2 * N * CAP, TOK).T
    hi = comb.astype(jnp.bfloat16)
    comb_hi[...] = hi
    comb_lo[...] = (comb - hi.astype(jnp.float32)).astype(jnp.bfloat16)

    def stage_a(j):
        for p in blocks_of(j):
            if DIST[p] != 0:
                dst = zin.at[:, pl.ds(p * CAP, CAP)]
                remote(dst, dst, zs.at[p], zr.at[p], dev(ctx_of(1), t)).wait_recv()

    def stage_x(j):
        rows = rows_of(j)
        for o in (2, 1, 3):
            to = chip(o)
            cp = remote(zin.at[to // 2, rows], xs.at[k, x, rows], xsend.at[j, o], xrecv.at[j, o], dev(c, 2 * to + k))
            cp.start()
            pending.append(cp)
        cp = remote(zin.at[group, rows], xs.at[k, x, rows], fs.at[j, 0], fr.at[j, 0], dev(c, mate))
        cp.start()
        pending.append(cp)
        xs[k, x, rows, :] = zin[group, rows, :]

    def stage_f(j):
        rows = rows_of(j)
        for o in (1, 3, 2):
            dst = xs.at[k, chip(NX - o), rows]
            remote(dst, dst, xsend.at[j, o], xrecv.at[j, o], dev(c, mate)).wait_recv()
            cp = remote(dst, dst, fs.at[j, o], fr.at[j, o], dev(c, mate))
            cp.start()
            pending.append(cp)

    def stage_b(j):
        rows = rows_of(j)
        if j == 0:
            wcopies[0].wait()
            wcopies[1].wait()

        def gate_up(parity):
            g_acc = u_acc = None
            nt = (((1,), (1,)), ((), ()))
            for xq in range(NX):
                a = xs[parity, xq, rows, :]
                cols = pl.ds(pl.multiple_of((2 * xq + parity) * FS, FS), FS)
                g_new = lax.dot_general(a, gate_v[:, cols], nt, preferred_element_type=jnp.float32)
                u_new = lax.dot_general(a, up_v[:, cols], nt, preferred_element_type=jnp.float32)
                g_acc = g_new if g_acc is None else g_acc + g_new
                u_acc = u_new if u_acc is None else u_acc + u_new
            return g_acc, u_acc

        g_mine, u_mine = gate_up(k)
        for o in range(NX):
            dst = xs.at[1 - k, chip(NX - o), rows]
            remote(dst, dst, fs.at[j, o], fr.at[j, o], dev(c, mate)).wait_recv()
        g_mate, u_mate = gate_up(1 - k)
        g_acc, u_acc = g_mine + g_mate, u_mine + u_mate
        hidden = (g_acc / (1.0 + jnp.exp(-g_acc)) * u_acc).astype(jnp.bfloat16)
        if j == 0:
            wcopies[2].wait()

        def down(xq, parity):
            cols = pl.ds(pl.multiple_of((2 * xq + parity) * FS, FS), FS)
            return jnp.dot(hidden, down_v[:, cols], preferred_element_type=jnp.float32)

        for xq in range(NX):
            mate_s[xq, rows, :] = down(xq, 1 - k).astype(jnp.bfloat16)
        cp = remote(mate_s.at[:, rows], mate_r.at[:, rows], ms.at[j], mr.at[j], dev(c, mate))
        cp.start()
        pending.append(cp)
        for o in range(NX):
            own[o, rows, :] = down(chip(o), k)

    def stage_c(j):
        rows = rows_of(j)
        remote(mate_s.at[:, rows], mate_r.at[:, rows], ms.at[j], mr.at[j], dev(c, mate)).wait_recv()
        for o in (2, 1, 3):
            to = chip(o)
            chip_s[o, rows, :] = (own[o, rows, :] + mate_r[to, rows, :].astype(jnp.float32)).astype(jnp.bfloat16)
            cp = remote(chip_s.at[o, rows], chip_r.at[x, rows], ps.at[j, o], pr.at[j, o], dev(c, 2 * to + k))
            cp.start()
            pending.append(cp)
        own[0, rows, :] = own[0, rows, :] + mate_r[x, rows, :].astype(jnp.float32)

    def stage_d(j):
        rows = rows_of(j)
        for o in (1, 3, 2):
            dst = chip_r.at[chip(NX - o), rows]
            remote(dst, dst, ps.at[j, o], pr.at[j, o], dev(c, mate)).wait_recv()
        pair = x + 1 - 2 * (x % 2)
        far = 2 * (1 - group)
        ret[group, rows, :] = (own[0, rows, :] + chip_r[pair, rows, :].astype(jnp.float32)).astype(jnp.bfloat16)
        ret[1 - group, rows, :] = (chip_r[far, rows, :].astype(jnp.float32)
                                   + chip_r[far + 1, rows, :].astype(jnp.float32)).astype(jnp.bfloat16)
        for p in blocks_of(j):
            q, d = BACK[p], DIST[p]
            src, dst = ret.at[:, pl.ds(p * CAP, CAP)], back.at[:, pl.ds(q * CAP, CAP)]
            if d == 0:
                dst[...] = src[...]
                continue
            cp = remote(src, dst, rs.at[p], rr.at[q], dev(ctx_of(d), t))
            cp.start()
            pending.append(cp)

    stages = {"A": stage_a, "X": stage_x, "F": stage_f, "B": stage_b, "C": stage_c, "D": stage_d, "S": dispatch}
    for step in ORDER:
        stages[step[0]](int(step[1]))

    total = None
    half = N // 2
    for h in range(2):
        for p in range(h * half, (h + 1) * half):
            if DIST[p] != 0:
                dst = back.at[:, pl.ds(p * CAP, CAP)]
                remote(dst, dst, rs.at[p], rr.at[p], dev(ctx_of(1), t)).wait_recv()
        for g in range(2):
            piece = back[g, h * half * CAP:(h + 1) * half * CAP, :]
            first = g * N * CAP + h * half * CAP
            cols = slice(first, first + half * CAP)
            part = (jnp.dot(comb_hi[:, cols], piece, preferred_element_type=jnp.float32)
                    + jnp.dot(comb_lo[:, cols], piece, preferred_element_type=jnp.float32))
            total = part if total is None else total + part
    out[...] = total.astype(jnp.bfloat16)
    for cp in pending:
        cp.wait_send()


def shards(tokens, expert_ids, route_weight, gate_weight, up_weight, down_weight):
    bf, f32 = jnp.bfloat16, jnp.float32
    vmem, dma = pltpu.VMEM, pltpu.SemaphoreType.DMA
    full = pl.BlockSpec(memory_space=pltpu.VMEM)
    hbm = pl.BlockSpec(memory_space=pltpu.HBM)
    return pl.pallas_call(
        kernel,
        out_shape=jax.ShapeDtypeStruct((TOK, FS), bf),
        in_specs=[hbm] * 6,
        out_specs=full,
        scratch_shapes=[
            vmem((TOK, FS), bf), vmem((TOP, TOK), jnp.int32), vmem((TOP, TOK), f32),
            vmem((2, N * CAP, FS), bf), vmem((2, NX, N * CAP, FS), bf),
            vmem((FQ, NS * FS), bf), vmem((FQ, NS * FS), bf), vmem((FQ, NS * FS), bf),
            vmem((2, N * CAP, FS), bf), vmem((TOK, 2 * N * CAP), bf), vmem((TOK, 2 * N * CAP), bf),
            vmem((2, N * CAP, FS), bf),
            vmem((NX, N * CAP, FS), f32),
            vmem((NX, N * CAP, FS), bf), vmem((NX, N * CAP, FS), bf),
            vmem((NX, N * CAP, FS), bf), vmem((NX, N * CAP, FS), bf), vmem((2, N * CAP, FS), bf),
            dma((6,)), dma((N,)), dma((N,)), dma((NCH, NX)), dma((NCH, NX)), dma((NCH, NX)), dma((NCH, NX)),
            dma((NCH,)), dma((NCH,)), dma((NCH, NX)), dma((NCH, NX)), dma((N,)), dma((N,)),
        ],
        compiler_params=pltpu.CompilerParams(collective_id=0, has_side_effects=True, vmem_limit_bytes=60 << 20),
    )(tokens, expert_ids.T, route_weight.T, gate_weight[0], up_weight[0], down_weight[0])


def solution(mesh):
    return jax.shard_map(
        shards,
        mesh=mesh,
        in_specs=(
            P(("dp", "ctx"), "tp"),
            P(("dp", "ctx"), None),
            P(("dp", "ctx"), None),
            P(("ctx", "tp"), None, None),
            P(("ctx", "tp"), None, None),
            P(("ctx", "tp"), None, None),
        ),
        out_specs=P(("dp", "ctx"), "tp"),
        check_vma=False,
    )
```
